32 devices in a mesh: front: 2 (over x), row: 4 (over y, core), col: 4 (over z).
Axes of the slice: x: 2, y: 2, z: 4, core: 2. Of those that a mesh axis runs over, the one named last changes fastest.
Arguments:
- child_fronts: float32 [32, 1536, 1536], P(('front', 'row', 'col')), may hold values from -6 to 103.97959, as said below
- parent_entries: float32 [2, 4096, 4096], P('front', 'row', 'col'), may hold values from -6 to 166, as said below
- tile_map: int32 [32, 8], P(('front', 'row', 'col')), may hold values from 0 to 31, as said below
- parent_group: int32 [32], P(('front', 'row', 'col')), may hold values from 0 to 1, as said below
Outputs:
- child_factor: float32 [32, 1536, 512], P(('front', 'row', 'col'))
- parent_factor: float32 [2, 4096, 4096], P('front', 'row', 'col')
The draws below stay inside these ranges and needn't reach their ends.
Inputs may be any that keep to these rules, and one draw needn't show every extreme that they name: `child_fronts`: each child front is symmetric positive definite. `parent_entries`: each parent's entries are symmetric, and every assembled parent front is positive definite. `tile_map`: each row is increasing and names exactly 2 tiles among each 8 consecutive tile numbers that start at a multiple of 8. `parent_group`: children are numbered in the order of the devices; in each run of 16 consecutive children, exactly 8 have each parent.
All inputs are finite; a program needn't handle non-finite values.
Results may differ from the reference program's by a relative error of at most 0.0001.
Values sent between devices are 32-bit elements; how exact they have to be, the bound alone decides.
A program may use at most 192 MiB of HBM per device.

```python
import jax
import jax.numpy as jnp
from jax import lax

TILE = 128
K = 512
B = 1024
P_SIZE = 4096
E = 1024
G = 2
CHILDREN = 32
BT = 8
PTD = 8
MAPPER = 2
NPER = 8
N_ROW = 4


def symmetric_front(key, count, order):
    noise = jnp.clip(jax.random.normal(key, (count, order, order), jnp.float32), -4.0, 4.0)
    symmetric = (noise + jnp.swapaxes(noise, 1, 2)) * 0.70710678
    return symmetric + 2.5 * order ** 0.5 * jnp.eye(order, dtype=jnp.float32)[None]


def draw_child_fronts(key, part):
    return symmetric_front(jax.random.fold_in(key, 11), CHILDREN, K + B)


def draw_parent_entries(key, part):
    return symmetric_front(jax.random.fold_in(key, 23), G, P_SIZE)


def draw_tile_map(key, part):
    keys_list = jax.random.split(jax.random.fold_in(key, 37), CHILDREN * N_ROW)

    def choose(one_key):
        return jnp.sort(jax.random.permutation(one_key, PTD)[:MAPPER])
    picked = jax.vmap(choose)(keys_list).reshape(CHILDREN, N_ROW, MAPPER).astype(jnp.int32)
    starts = (jnp.arange(N_ROW, dtype=jnp.int32) * PTD)[None, :, None]
    return (picked + starts).reshape(CHILDREN, BT)


def draw_parent_group(key, part):
    slices = CHILDREN // (NPER * G)
    keys_list = jax.random.split(jax.random.fold_in(key, 53), slices)
    pattern = jnp.repeat(jnp.arange(G, dtype=jnp.int32), NPER)

    def shuffle(one_key):
        return jax.random.permutation(one_key, pattern)
    return jax.vmap(shuffle)(keys_list).reshape(CHILDREN).astype(jnp.int32)


def setup_inputs(seed: int = 0) -> dict:
    keys = jax.random.split(jax.random.key(seed), 5)
    return {
        "child_fronts": draw_child_fronts(jax.random.fold_in(keys[4], 71), 0),
        "parent_entries": draw_parent_entries(jax.random.fold_in(keys[4], 71), 0),
        "tile_map": draw_tile_map(jax.random.fold_in(keys[4], 71), 0),
        "parent_group": draw_parent_group(jax.random.fold_in(keys[4], 71), 0),
    }


def right_solve(pivot_factor, matrix):
    return lax.linalg.triangular_solve(pivot_factor, matrix, left_side=False, lower=True, transpose_a=True)

def factor_child(child_front):
    corner = child_front[:K, :K]
    border_cols = child_front[K:, :K]
    border_block = child_front[K:, K:]
    pivot_factor = jnp.linalg.cholesky(corner)
    child_panel = right_solve(pivot_factor, border_cols)
    update = border_block - jnp.dot(child_panel, child_panel.T, precision=lax.Precision.HIGHEST)
    return (jnp.concatenate([pivot_factor, child_panel], 0), update)

def eliminate(assembled):
    pivot_factor = jnp.linalg.cholesky(assembled[:E, :E])
    panel = right_solve(pivot_factor, assembled[E:, :E])
    trailing = assembled[E:, E:] - jnp.dot(panel, panel.T, precision=lax.Precision.HIGHEST)
    upper = jnp.concatenate([pivot_factor, panel.T], 1)
    bottom = jnp.concatenate([panel, trailing], 1)
    return jnp.concatenate([upper, bottom], 0)

def reference(child_fronts, parent_entries, tile_map, parent_group):
    offsets = jnp.arange(TILE, dtype=jnp.int32)

    def one_child(child, carry):
        parents, factors = carry
        factor, update = factor_child(child_fronts[child])
        factors = factors.at[child].set(factor)
        row_index = (tile_map[child][:, None] * TILE + offsets[None, :]).reshape(-1).astype(jnp.int32)
        parent_id = parent_group[child]
        parents = parents.at[parent_id, row_index[:, None], row_index[None, :]].add(update)
        return (parents, factors)
    factors = jnp.zeros((CHILDREN, K + B, K), jnp.float32)
    parents, factors = lax.fori_loop(0, CHILDREN, one_child, (parent_entries, factors))
    return (factors, lax.map(eliminate, parents))
```

```python
import functools

import jax
import jax.numpy as jnp
from jax import lax
from jax.experimental import pallas as pl
from jax.experimental.pallas import tpu as pltpu
from jax.sharding import PartitionSpec as P

TILE = 128
NB = 16
F32 = jnp.float32
BF16 = jnp.bfloat16
NT = (((1,), (1,)), ((), ()))
TN = (((0,), (0,)), ((), ()))
PARAMS = pltpu.CompilerParams(vmem_limit_bytes=56 * 1024 * 1024)
VMEM = pl.BlockSpec(memory_space=pltpu.VMEM)
SMEM = pl.BlockSpec(memory_space=pltpu.SMEM)


def split(x):
    hi = x.astype(BF16)
    return hi, (x - hi.astype(F32)).astype(BF16)


def mxu(a, b, dims):
    return lax.dot_general(a, b, dims, preferred_element_type=F32)


def weights(hi, lo):
    top = jnp.concatenate([hi, hi], 1)
    return jnp.concatenate([top, jnp.concatenate([lo, jnp.zeros_like(lo)], 1)], 0)


def product(hi, lo, weight):
    both = mxu(jnp.concatenate([hi, lo], 1), weight, NT)
    return both[:, :TILE] + both[:, TILE:]


def product3(ah, al, bh, bl):
    return mxu(ah, bh, NT) + mxu(ah, bl, NT) + mxu(al, bh, NT)


def chol_inverse(work):
    rows = lax.broadcasted_iota(jnp.int32, (NB, TILE), 0)
    for start in range(0, TILE, NB):
        left = work[start : start + NB, :TILE]
        right = work[start : start + NB, TILE:]
        cols = [
            jnp.broadcast_to(left[:, start + b : start + b + 1], (NB, TILE)) for b in range(NB)
        ]
        for a in range(NB):
            scale = lax.rsqrt(cols[a][a : a + 1, :])
            factor = jnp.where(rows > a, cols[a] * scale, 0.0)
            pivot_left = left[a : a + 1, :] * scale
            pivot_right = right[a : a + 1, :] * scale
            left = jnp.where(rows == a, pivot_left, left - factor * pivot_left)
            right = jnp.where(rows == a, pivot_right, right - factor * pivot_right)
            for b in range(a + 1, NB):
                cols[b] = cols[b] - factor * (cols[b][a : a + 1, :] * scale)
        work[start : start + NB, :TILE] = left
        work[start : start + NB, TILE:] = right
        if start + NB < TILE:
            hi, lo = split(jnp.concatenate([left, right], 1))
            mine = jnp.concatenate([hi[:, :TILE], hi[:, :TILE], lo[:, :TILE]], 0)
            change = mxu(mine, jnp.concatenate([hi, lo, hi], 0), TN)
            work[start + NB :, :] = work[start + NB :, :] - change[start + NB :, :]


def factor_loop(src, out, hi, lo, inv_hi, inv_lo, work, col, blocks, chunk):
    total = src.shape[0]
    row_id = lax.broadcasted_iota(jnp.int32, (TILE, TILE), 0)
    col_id = lax.broadcasted_iota(jnp.int32, (TILE, TILE), 1)

    def step(k, carry):
        here = pl.ds(pl.multiple_of(k * TILE, TILE), TILE)
        col[...] = src[:, here]

        def earlier(m, carry):
            there = pl.ds(pl.multiple_of(m * TILE, TILE), TILE)
            weight = weights(hi[here, there], lo[here, there])
            for first in range(0, total, chunk):
                part = pl.ds(first, chunk)
                col[part, :] = col[part, :] - product(hi[part, there], lo[part, there], weight)
            return carry

        lax.fori_loop(0, k, earlier, 0)
        work[:, :TILE] = col[here, :]
        work[:, TILE:] = jnp.where(row_id == col_id, 1.0, 0.0).astype(F32)
        chol_inverse(work)
        inverse_hi, inverse_lo = split(work[:, TILE:])
        if inv_hi is not None:
            inv_hi[k] = inverse_hi
            inv_lo[k] = inverse_lo
        weight = weights(inverse_hi, inverse_lo)
        for first in range(0, total, chunk):
            part = pl.ds(first, chunk)
            a_hi, a_lo = split(col[part, :])
            panel = product(a_hi, a_lo, weight)
            ids = lax.broadcasted_iota(jnp.int32, (chunk, TILE), 0) + first
            panel = jnp.where(ids >= k * TILE, panel, 0.0)
            out[part, here] = panel
            p_hi, p_lo = split(panel)
            hi[part, here] = p_hi
            lo[part, here] = p_lo
        lower = jnp.where(row_id >= col_id, work[:, :TILE].T, 0.0)
        out[here, here] = lower
        d_hi, d_lo = split(lower)
        hi[here, here] = d_hi
        lo[here, here] = d_lo
        return carry

    lax.fori_loop(0, blocks, step, 0)


def child_kernel(row_count, col_count, front, factor, pieces, hi, lo, work, col):
    pivots = factor.shape[1]
    factor_loop(front, factor, hi, lo, None, None, work, col, pivots // TILE, 512)
    size = pieces.shape[1]

    def piece(index, carry):
        i = index // col_count
        j = index % col_count
        a = pl.ds(pl.multiple_of(pivots + i * size, TILE), size)
        b = pl.ds(pl.multiple_of(pivots + j * size, TILE), size)
        pieces[index] = front[a, b] - product3(hi[a, :], lo[a, :], hi[b, :], lo[b, :])
        return carry

    lax.fori_loop(0, row_count * col_count, piece, 0)


def child_call(front, border, row_count, col_count):
    order = front.shape[0]
    pivots = order - border
    size = border // row_count
    return pl.pallas_call(
        functools.partial(child_kernel, row_count, col_count),
        out_shape=(
            jax.ShapeDtypeStruct((order, pivots), F32),
            jax.ShapeDtypeStruct((row_count * col_count, size, size), F32),
        ),
        in_specs=[VMEM],
        out_specs=(VMEM, VMEM),
        scratch_shapes=[
            pltpu.VMEM((order, pivots), BF16),
            pltpu.VMEM((order, pivots), BF16),
            pltpu.VMEM((TILE, 2 * TILE), F32),
            pltpu.VMEM((order, TILE), F32),
        ],
        compiler_params=PARAMS,
        name="child",
    )(front)


def reorder_kernel(order, source, target):
    target[...] = source[...]


def reorder_call(order, pieces):
    shape = (1,) + pieces.shape[1:]
    return pl.pallas_call(
        reorder_kernel,
        out_shape=jax.ShapeDtypeStruct(pieces.shape, F32),
        grid_spec=pltpu.PrefetchScalarGridSpec(
            num_scalar_prefetch=1,
            grid=(pieces.shape[0],),
            in_specs=[pl.BlockSpec(shape, lambda i, order: (order[i], 0, 0))],
            out_specs=pl.BlockSpec(shape, lambda i, order: (i, 0, 0)),
        ),
        name="reorder",
    )(order, pieces)


def assemble_kernel(row_tiles, col_tiles, block, pieces, out):
    out[...] = block[...]
    per_block = row_tiles.shape[1]

    def add(index, carry):
        for i in range(per_block):
            for j in range(per_block):
                r = pl.ds(pl.multiple_of(row_tiles[index, i] * TILE, TILE), TILE)
                c = pl.ds(pl.multiple_of(col_tiles[index, j] * TILE, TILE), TILE)
                tile = pieces[index, i * TILE : (i + 1) * TILE, j * TILE : (j + 1) * TILE]
                out[r, c] = out[r, c] + tile
        return carry

    lax.fori_loop(0, pieces.shape[0], add, 0)


def assemble_call(row_tiles, col_tiles, block, pieces):
    return pl.pallas_call(
        assemble_kernel,
        out_shape=jax.ShapeDtypeStruct(block.shape, F32),
        in_specs=[SMEM, SMEM, VMEM, VMEM],
        out_specs=VMEM,
        compiler_params=PARAMS,
        name="assemble",
    )(row_tiles, col_tiles, block, pieces)


def corner_kernel(src, out, hi, lo, inv_hi, inv_lo, work, col):
    factor_loop(
        src, out, hi, lo, inv_hi, inv_lo, work, col, src.shape[1] // TILE, src.shape[0] // 2
    )


def corner_call(src):
    order = src.shape[0]
    blocks = order // TILE
    return pl.pallas_call(
        corner_kernel,
        out_shape=(
            jax.ShapeDtypeStruct((order, order), F32),
            jax.ShapeDtypeStruct((order, order), BF16),
            jax.ShapeDtypeStruct((order, order), BF16),
            jax.ShapeDtypeStruct((blocks, TILE, TILE), BF16),
            jax.ShapeDtypeStruct((blocks, TILE, TILE), BF16),
        ),
        in_specs=[VMEM],
        out_specs=(VMEM,) * 5,
        scratch_shapes=[pltpu.VMEM((TILE, 2 * TILE), F32), pltpu.VMEM((order, TILE), F32)],
        compiler_params=PARAMS,
        name="corner",
    )(src)


def finish_kernel(place, block, left, top, corner, hi, lo, inv_hi, inv_lo, out, panel, p_hi, p_lo):
    order = block.shape[0]
    count = order // TILE
    half = order // 2

    def turn(k, carry):
        here = pl.ds(pl.multiple_of(k * TILE, TILE), TILE)
        panel[:order, here] = left[:, here]
        for m in range(count):
            panel[order + m * TILE : order + (m + 1) * TILE, here] = top[
                here, m * TILE : (m + 1) * TILE
            ].T
        return carry

    lax.fori_loop(0, count, turn, 0)

    def step(k, carry):
        here = pl.ds(pl.multiple_of(k * TILE, TILE), TILE)

        def earlier(m, carry):
            there = pl.ds(pl.multiple_of(m * TILE, TILE), TILE)
            weight = weights(hi[here, there], lo[here, there])
            for first in range(0, 2 * order, half):
                part = pl.ds(first, half)
                change = product(p_hi[part, there], p_lo[part, there], weight)
                panel[part, here] = panel[part, here] - change
            return carry

        lax.fori_loop(0, k, earlier, 0)
        weight = weights(inv_hi[k], inv_lo[k])
        for first in range(0, 2 * order, half):
            part = pl.ds(first, half)
            a_hi, a_lo = split(panel[part, here])
            solved = product(a_hi, a_lo, weight)
            panel[part, here] = solved
            s_hi, s_lo = split(solved)
            p_hi[part, here] = s_hi
            p_lo[part, here] = s_lo
        return carry

    lax.fori_loop(0, count, step, 0)
    row = place[0]
    column = place[1]

    @pl.when((row == 0) & (column == 0))
    def _():
        out[...] = corner[...]

    @pl.when((row > 0) & (column == 0))
    def _():
        out[...] = panel[:order, :]

    @pl.when((row == 0) & (column > 0))
    def _():
        def back(k, carry):
            here = pl.ds(pl.multiple_of(k * TILE, TILE), TILE)
            for m in range(count):
                out[here, m * TILE : (m + 1) * TILE] = panel[
                    order + m * TILE : order + (m + 1) * TILE, here
                ].T
            return carry

        lax.fori_loop(0, count, back, 0)

    @pl.when((row > 0) & (column > 0))
    def _():
        size = 2 * TILE
        across = order // size

        def trail(index, carry):
            i = index // across
            j = index % across
            a = pl.ds(pl.multiple_of(i * size, size), size)
            b = pl.ds(pl.multiple_of(j * size, size), size)
            c = pl.ds(pl.multiple_of(order + j * size, size), size)
            out[a, b] = block[a, b] - product3(p_hi[a, :], p_lo[a, :], p_hi[c, :], p_lo[c, :])
            return carry

        lax.fori_loop(0, across * across, trail, 0)


def finish_call(place, block, left, top, corner, hi, lo, inv_hi, inv_lo):
    order = block.shape[0]
    return pl.pallas_call(
        finish_kernel,
        out_shape=jax.ShapeDtypeStruct(block.shape, F32),
        in_specs=[SMEM] + [VMEM] * 8,
        out_specs=VMEM,
        scratch_shapes=[
            pltpu.VMEM((2 * order, order), F32),
            pltpu.VMEM((2 * order, order), BF16),
            pltpu.VMEM((2 * order, order), BF16),
        ],
        compiler_params=PARAMS,
        name="finish",
    )(place, block, left, top, corner, hi, lo, inv_hi, inv_lo)


def broadcast(array, axis, root):
    mine = lax.axis_index(axis) == root
    return lax.psum(jnp.where(mine, array, jnp.zeros_like(array)), axis)


def local(child_fronts, parent_entries, tile_map, parent_group):
    border_tiles = tile_map.shape[1]
    border = border_tiles * TILE
    row_count = lax.axis_size("row")
    col_count = lax.axis_size("col")
    front_count = lax.axis_size("front")
    row_here = lax.axis_index("row")
    col_here = lax.axis_index("col")
    front_here = lax.axis_index("front")
    group_size = row_count * col_count

    labels = jnp.concatenate([tile_map, parent_group[:, None]], 1)
    labels = lax.all_gather(labels, ("front", "row", "col"), axis=0, tiled=True)
    labels = labels.reshape(front_count, group_size, border_tiles + 1)
    groups = labels[:, :, border_tiles]
    number = jnp.arange(group_size, dtype=jnp.int32)
    ahead = (groups[:, None, :] < groups[:, :, None]) | (
        (groups[:, None, :] == groups[:, :, None]) & (number[None, None, :] < number[None, :, None])
    )
    rank = jnp.sum(ahead.astype(jnp.int32), 2)
    chosen = rank[:, None, :] == number[None, :, None]
    arrange = jnp.sum(jnp.where(chosen, number[None, None, :], 0), 2)
    per_parent = group_size // front_count
    ids = jnp.sum(
        jnp.where(chosen[:, :, :, None], labels[:, None, :, :border_tiles], 0), 2
    ).reshape(front_count, front_count, per_parent, border_tiles)
    ids = lax.dynamic_index_in_dim(ids, front_here, 1, False).reshape(-1, border_tiles)
    my_order = lax.dynamic_index_in_dim(arrange, front_here, 0, False)

    factor, pieces = child_call(child_fronts[0], border, row_count, col_count)
    size = border // row_count
    arrived = lax.all_to_all(pieces, ("row", "col"), split_axis=0, concat_axis=0, tiled=True)
    regrouped = reorder_call(my_order, arrived).reshape(front_count, per_parent, size, size)
    landed = lax.all_to_all(regrouped, "front", split_axis=0, concat_axis=0, tiled=True)
    landed = landed.reshape(-1, size, size)

    block = parent_entries[0]
    local_tiles = block.shape[0] // TILE
    per_block = border_tiles // row_count
    row_tiles = (
        lax.dynamic_slice_in_dim(ids, row_here * per_block, per_block, 1) - row_here * local_tiles
    )
    col_tiles = (
        lax.dynamic_slice_in_dim(ids, col_here * per_block, per_block, 1) - col_here * local_tiles
    )
    block = assemble_call(row_tiles, col_tiles, block, landed)
    diag = broadcast(block, ("row", "col"), 0)
    left = broadcast(block, "col", 0)
    top = broadcast(block, "row", 0)
    corner, hi, lo, inv_hi, inv_lo = corner_call(diag)
    place = jnp.stack([row_here, col_here]).astype(jnp.int32)
    result = finish_call(place, block, left, top, corner, hi, lo, inv_hi, inv_lo)
    return (factor[None], result[None])


def solution(mesh):
    in_specs = (
        P(("front", "row", "col"), None, None),
        P("front", "row", "col"),
        P(("front", "row", "col"), None),
        P(("front", "row", "col")),
    )
    out_specs = (P(("front", "row", "col"), None, None), P("front", "row", "col"))
    return jax.shard_map(local, mesh=mesh, in_specs=in_specs, out_specs=out_specs, check_vma=False)
```

```python
import functools

import jax
import jax.numpy as jnp
from jax import lax
from jax.experimental import pallas as pl
from jax.experimental.pallas import tpu as pltpu
from jax.sharding import PartitionSpec as P

TILE = 128
NB = 16
F32 = jnp.float32
BF16 = jnp.bfloat16
NT = (((1,), (1,)), ((), ()))
TN = (((0,), (0,)), ((), ()))
PARAMS = pltpu.CompilerParams(vmem_limit_bytes=56 * 1024 * 1024)
VMEM = pl.BlockSpec(memory_space=pltpu.VMEM)
SMEM = pl.BlockSpec(memory_space=pltpu.SMEM)


def split(x):
    hi = x.astype(BF16)
    return hi, (x - hi.astype(F32)).astype(BF16)


def mxu(a, b, dims):
    return lax.dot_general(a, b, dims, preferred_element_type=F32)


def weights(hi, lo):
    top = jnp.concatenate([hi, hi], 1)
    return jnp.concatenate([top, jnp.concatenate([lo, jnp.zeros_like(lo)], 1)], 0)


def product(hi, lo, weight):
    both = mxu(jnp.concatenate([hi, lo], 1), weight, NT)
    return both[:, :TILE] + both[:, TILE:]


def product3(ah, al, bh, bl):
    return mxu(ah, bh, NT) + mxu(ah, bl, NT) + mxu(al, bh, NT)


def chol_inverse(work):
    rows = lax.broadcasted_iota(jnp.int32, (NB, TILE), 0)
    for start in range(0, TILE, NB):
        left = work[start : start + NB, :TILE]
        right = work[start : start + NB, TILE:]
        cols = [
            jnp.broadcast_to(left[:, start + b : start + b + 1], (NB, TILE)) for b in range(NB)
        ]
        for a in range(NB):
            scale = lax.rsqrt(cols[a][a : a + 1, :])
            factor = jnp.where(rows > a, cols[a] * scale, 0.0)
            pivot_left = left[a : a + 1, :] * scale
            pivot_right = right[a : a + 1, :] * scale
            left = jnp.where(rows == a, pivot_left, left - factor * pivot_left)
            right = jnp.where(rows == a, pivot_right, right - factor * pivot_right)
            for b in range(a + 1, NB):
                cols[b] = cols[b] - factor * (cols[b][a : a + 1, :] * scale)
        work[start : start + NB, :TILE] = left
        work[start : start + NB, TILE:] = right
        if start + NB < TILE:
            hi, lo = split(jnp.concatenate([left, right], 1))
            mine = jnp.concatenate([hi[:, :TILE], hi[:, :TILE], lo[:, :TILE]], 0)
            change = mxu(mine, jnp.concatenate([hi, lo, hi], 0), TN)
            work[start + NB :, :] = work[start + NB :, :] - change[start + NB :, :]


def factor_loop(src, out, hi, lo, inv_hi, inv_lo, work, col, blocks, chunk):
    total = src.shape[0]
    row_id = lax.broadcasted_iota(jnp.int32, (TILE, TILE), 0)
    col_id = lax.broadcasted_iota(jnp.int32, (TILE, TILE), 1)

    def step(k, carry):
        here = pl.ds(pl.multiple_of(k * TILE, TILE), TILE)
        col[...] = src[:, here]

        def earlier(m, carry):
            there = pl.ds(pl.multiple_of(m * TILE, TILE), TILE)
            weight = weights(hi[here, there], lo[here, there])
            for first in range(0, total, chunk):
                part = pl.ds(first, chunk)
                col[part, :] = col[part, :] - product(hi[part, there], lo[part, there], weight)
            return carry

        lax.fori_loop(0, k, earlier, 0)
        work[:, :TILE] = col[here, :]
        work[:, TILE:] = jnp.where(row_id == col_id, 1.0, 0.0).astype(F32)
        chol_inverse(work)
        inverse_hi, inverse_lo = split(work[:, TILE:])
        if inv_hi is not None:
            inv_hi[k] = inverse_hi
            inv_lo[k] = inverse_lo
        weight = weights(inverse_hi, inverse_lo)
        for first in range(0, total, chunk):
            part = pl.ds(first, chunk)
            a_hi, a_lo = split(col[part, :])
            panel = product(a_hi, a_lo, weight)
            ids = lax.broadcasted_iota(jnp.int32, (chunk, TILE), 0) + first
            panel = jnp.where(ids >= k * TILE, panel, 0.0)
            out[part, here] = panel
            p_hi, p_lo = split(panel)
            hi[part, here] = p_hi
            lo[part, here] = p_lo
        lower = jnp.where(row_id >= col_id, work[:, :TILE].T, 0.0)
        out[here, here] = lower
        d_hi, d_lo = split(lower)
        hi[here, here] = d_hi
        lo[here, here] = d_lo
        return carry

    lax.fori_loop(0, blocks, step, 0)


def child_kernel(row_count, col_count, front, factor, pieces, hi, lo, work, col):
    pivots = factor.shape[1]
    factor_loop(front, factor, hi, lo, None, None, work, col, pivots // TILE, 512)
    size = pieces.shape[1]

    def piece(index, carry):
        i = index // col_count
        j = index % col_count
        a = pl.ds(pl.multiple_of(pivots + i * size, TILE), size)
        b = pl.ds(pl.multiple_of(pivots + j * size, TILE), size)
        pieces[index] = front[a, b] - product3(hi[a, :], lo[a, :], hi[b, :], lo[b, :])
        return carry

    lax.fori_loop(0, row_count * col_count, piece, 0)


def child_call(front, border, row_count, col_count):
    order = front.shape[0]
    pivots = order - border
    size = border // row_count
    return pl.pallas_call(
        functools.partial(child_kernel, row_count, col_count),
        out_shape=(
            jax.ShapeDtypeStruct((order, pivots), F32),
            jax.ShapeDtypeStruct((row_count * col_count, size, size), F32),
        ),
        in_specs=[VMEM],
        out_specs=(VMEM, VMEM),
        scratch_shapes=[
            pltpu.VMEM((order, pivots), BF16),
            pltpu.VMEM((order, pivots), BF16),
            pltpu.VMEM((TILE, 2 * TILE), F32),
            pltpu.VMEM((order, TILE), F32),
        ],
        compiler_params=PARAMS,
        name="child",
    )(front)


def reorder_kernel(order, source, target):
    target[...] = source[...]


def reorder_call(order, pieces):
    shape = (1,) + pieces.shape[1:]
    return pl.pallas_call(
        reorder_kernel,
        out_shape=jax.ShapeDtypeStruct(pieces.shape, F32),
        grid_spec=pltpu.PrefetchScalarGridSpec(
            num_scalar_prefetch=1,
            grid=(pieces.shape[0],),
            in_specs=[pl.BlockSpec(shape, lambda i, order: (order[i], 0, 0))],
            out_specs=pl.BlockSpec(shape, lambda i, order: (i, 0, 0)),
        ),
        name="reorder",
    )(order, pieces)


def assemble_kernel(place, row_tiles, col_tiles, block, pieces, out, turned):
    out[...] = block[...]
    per_block = row_tiles.shape[1]

    def add(index, carry):
        for i in range(per_block):
            for j in range(per_block):
                r = pl.ds(pl.multiple_of(row_tiles[index, i] * TILE, TILE), TILE)
                c = pl.ds(pl.multiple_of(col_tiles[index, j] * TILE, TILE), TILE)
                tile = pieces[index, i * TILE : (i + 1) * TILE, j * TILE : (j + 1) * TILE]
                out[r, c] = out[r, c] + tile
        return carry

    lax.fori_loop(0, pieces.shape[0], add, 0)
    turned[...] = jnp.zeros_like(turned)

    @pl.when(place[0] == 0)
    def _():
        count = out.shape[0] // TILE

        def turn(k, carry):
            here = pl.ds(pl.multiple_of(k * TILE, TILE), TILE)
            for m in range(count):
                turned[m * TILE : (m + 1) * TILE, here] = out[here, m * TILE : (m + 1) * TILE].T
            return carry

        lax.fori_loop(0, count, turn, 0)


def assemble_call(place, row_tiles, col_tiles, block, pieces):
    return pl.pallas_call(
        assemble_kernel,
        out_shape=(jax.ShapeDtypeStruct(block.shape, F32),) * 2,
        in_specs=[SMEM, SMEM, SMEM, VMEM, VMEM],
        out_specs=(VMEM, VMEM),
        compiler_params=PARAMS,
        name="assemble",
    )(place, row_tiles, col_tiles, block, pieces)


def corner_kernel(src, out, hi, lo, inv_hi, inv_lo, work, col):
    factor_loop(
        src, out, hi, lo, inv_hi, inv_lo, work, col, src.shape[1] // TILE, src.shape[0] // 2
    )


def corner_call(src):
    order = src.shape[0]
    blocks = order // TILE
    return pl.pallas_call(
        corner_kernel,
        out_shape=(
            jax.ShapeDtypeStruct((order, order), F32),
            jax.ShapeDtypeStruct((order, order), BF16),
            jax.ShapeDtypeStruct((order, order), BF16),
            jax.ShapeDtypeStruct((blocks, TILE, TILE), BF16),
            jax.ShapeDtypeStruct((blocks, TILE, TILE), BF16),
        ),
        in_specs=[VMEM],
        out_specs=(VMEM,) * 5,
        scratch_shapes=[pltpu.VMEM((TILE, 2 * TILE), F32), pltpu.VMEM((order, TILE), F32)],
        compiler_params=PARAMS,
        name="corner",
    )(src)


def solve_kernel(left, top, hi, lo, inv_hi, inv_lo, panel, p_hi, p_lo):
    count = hi.shape[0] // TILE
    share = left.shape[0]
    panel[:share, :] = left[...]
    panel[share:, :] = top[...]

    def step(k, carry):
        here = pl.ds(pl.multiple_of(k * TILE, TILE), TILE)

        def earlier(m, carry):
            there = pl.ds(pl.multiple_of(m * TILE, TILE), TILE)
            weight = weights(hi[here, there], lo[here, there])
            panel[:, here] = panel[:, here] - product(p_hi[:, there], p_lo[:, there], weight)
            return carry

        lax.fori_loop(0, k, earlier, 0)
        a_hi, a_lo = split(panel[:, here])
        solved = product(a_hi, a_lo, weights(inv_hi[k], inv_lo[k]))
        panel[:, here] = solved
        s_hi, s_lo = split(solved)
        p_hi[:, here] = s_hi
        p_lo[:, here] = s_lo
        return carry

    lax.fori_loop(0, count, step, 0)


def solve_call(left, top, hi, lo, inv_hi, inv_lo):
    shape = (left.shape[0] + top.shape[0], left.shape[1])
    return pl.pallas_call(
        solve_kernel,
        out_shape=jax.ShapeDtypeStruct(shape, F32),
        in_specs=[VMEM] * 6,
        out_specs=VMEM,
        scratch_shapes=[pltpu.VMEM(shape, BF16), pltpu.VMEM(shape, BF16)],
        compiler_params=PARAMS,
        name="solve",
    )(left, top, hi, lo, inv_hi, inv_lo)


def gather_kernel(rows, cols, part, row_out, col_out, own, send_row, get_row, send_col, get_col):
    row = lax.axis_index("row")
    column = lax.axis_index("col")
    share = part.shape[0] - row_out.shape[0] // cols
    first = part.shape[0] - share
    barrier = pltpu.get_barrier_semaphore()
    for step in range(1, cols):
        peer = {"col": lax.rem(column + step, cols)}
        pl.semaphore_signal(barrier, inc=1, device_id=peer, device_id_type=pl.DeviceIdType.MESH)
    for step in range(1, rows):
        peer = {"row": lax.rem(row + step, rows)}
        pl.semaphore_signal(barrier, inc=1, device_id=peer, device_id_type=pl.DeviceIdType.MESH)
    pl.semaphore_wait(barrier, cols + rows - 2)
    copies = []
    for step in range(1, cols):
        copies.append(
            pltpu.make_async_remote_copy(
                src_ref=part.at[pl.ds(0, first)],
                dst_ref=row_out.at[pl.ds(pl.multiple_of(column * first, first), first)],
                send_sem=send_row.at[step - 1],
                recv_sem=get_row.at[step - 1],
                device_id={"col": lax.rem(column + step, cols)},
                device_id_type=pl.DeviceIdType.MESH,
            )
        )
    for step in range(1, rows):
        copies.append(
            pltpu.make_async_remote_copy(
                src_ref=part.at[pl.ds(first, share)],
                dst_ref=col_out.at[pl.ds(pl.multiple_of(row * share, share), share)],
                send_sem=send_col.at[step - 1],
                recv_sem=get_col.at[step - 1],
                device_id={"row": lax.rem(row + step, rows)},
                device_id_type=pl.DeviceIdType.MESH,
            )
        )
    for copy in copies:
        copy.start()
    mine = (
        pltpu.make_async_copy(
            part.at[pl.ds(0, first)],
            row_out.at[pl.ds(pl.multiple_of(column * first, first), first)],
            own.at[0],
        ),
        pltpu.make_async_copy(
            part.at[pl.ds(first, share)],
            col_out.at[pl.ds(pl.multiple_of(row * share, share), share)],
            own.at[1],
        ),
    )
    for copy in mine:
        copy.start()
    for copy in mine:
        copy.wait()
    for copy in copies:
        copy.wait()


def gather_call(part, order, rows, cols):
    anywhere = pl.BlockSpec(memory_space=pl.ANY)
    return pl.pallas_call(
        functools.partial(gather_kernel, rows, cols),
        out_shape=(jax.ShapeDtypeStruct((order, order), F32),) * 2,
        in_specs=[anywhere],
        out_specs=(anywhere, anywhere),
        scratch_shapes=[
            pltpu.SemaphoreType.DMA((2,)),
            pltpu.SemaphoreType.DMA((cols - 1,)),
            pltpu.SemaphoreType.DMA((cols - 1,)),
            pltpu.SemaphoreType.DMA((rows - 1,)),
            pltpu.SemaphoreType.DMA((rows - 1,)),
        ],
        compiler_params=pltpu.CompilerParams(
            collective_id=1, has_side_effects=True, vmem_limit_bytes=32 * 1024 * 1024
        ),
        name="gather",
    )(part)


def finish_kernel(place, block, across, down, corner, out):
    order = block.shape[0]
    count = order // TILE
    row = place[0]
    column = place[1]

    @pl.when((row == 0) & (column == 0))
    def _():
        out[...] = corner[...]

    @pl.when((row > 0) & (column == 0))
    def _():
        out[...] = across[...]

    @pl.when((row == 0) & (column > 0))
    def _():
        def back(k, carry):
            here = pl.ds(pl.multiple_of(k * TILE, TILE), TILE)
            for m in range(count):
                out[here, m * TILE : (m + 1) * TILE] = down[m * TILE : (m + 1) * TILE, here].T
            return carry

        lax.fori_loop(0, count, back, 0)

    @pl.when((row > 0) & (column > 0))
    def _():
        size = 2 * TILE
        wide = order // size

        def trail(index, carry):
            a = pl.ds(pl.multiple_of(index // wide * size, size), size)
            b = pl.ds(pl.multiple_of(index % wide * size, size), size)
            a_hi, a_lo = split(across[a, :])
            b_hi, b_lo = split(down[b, :])
            out[a, b] = block[a, b] - product3(a_hi, a_lo, b_hi, b_lo)
            return carry

        lax.fori_loop(0, wide * wide, trail, 0)


def finish_call(place, block, across, down, corner):
    return pl.pallas_call(
        finish_kernel,
        out_shape=jax.ShapeDtypeStruct(block.shape, F32),
        in_specs=[SMEM] + [VMEM] * 4,
        out_specs=VMEM,
        compiler_params=PARAMS,
        name="finish",
    )(place, block, across, down, corner)


def broadcast(array, axis, root):
    mine = lax.axis_index(axis) == root
    return lax.psum(jnp.where(mine, array, jnp.zeros_like(array)), axis)


def local(child_fronts, parent_entries, tile_map, parent_group):
    border_tiles = tile_map.shape[1]
    border = border_tiles * TILE
    row_count = lax.axis_size("row")
    col_count = lax.axis_size("col")
    front_count = lax.axis_size("front")
    row_here = lax.axis_index("row")
    col_here = lax.axis_index("col")
    front_here = lax.axis_index("front")
    group_size = row_count * col_count

    labels = jnp.concatenate([tile_map, parent_group[:, None]], 1)
    labels = lax.all_gather(labels, ("front", "row", "col"), axis=0, tiled=True)
    labels = labels.reshape(front_count, group_size, border_tiles + 1)
    groups = labels[:, :, border_tiles]
    number = jnp.arange(group_size, dtype=jnp.int32)
    ahead = (groups[:, None, :] < groups[:, :, None]) | (
        (groups[:, None, :] == groups[:, :, None]) & (number[None, None, :] < number[None, :, None])
    )
    rank = jnp.sum(ahead.astype(jnp.int32), 2)
    chosen = rank[:, None, :] == number[None, :, None]
    arrange = jnp.sum(jnp.where(chosen, number[None, None, :], 0), 2)
    per_parent = group_size // front_count
    ids = jnp.sum(
        jnp.where(chosen[:, :, :, None], labels[:, None, :, :border_tiles], 0), 2
    ).reshape(front_count, front_count, per_parent, border_tiles)
    ids = lax.dynamic_index_in_dim(ids, front_here, 1, False).reshape(-1, border_tiles)
    my_order = lax.dynamic_index_in_dim(arrange, front_here, 0, False)

    child, ids, my_order = lax.optimization_barrier((child_fronts[0], ids, my_order))
    factor, pieces = child_call(child, border, row_count, col_count)
    size = border // row_count
    arrived = lax.all_to_all(pieces, ("row", "col"), split_axis=0, concat_axis=0, tiled=True)
    regrouped = reorder_call(my_order, arrived).reshape(front_count, per_parent, size, size)
    landed = lax.all_to_all(regrouped, "front", split_axis=0, concat_axis=0, tiled=True)
    landed = landed.reshape(-1, size, size)

    block = parent_entries[0]
    local_tiles = block.shape[0] // TILE
    per_block = border_tiles // row_count
    row_tiles = (
        lax.dynamic_slice_in_dim(ids, row_here * per_block, per_block, 1) - row_here * local_tiles
    )
    col_tiles = (
        lax.dynamic_slice_in_dim(ids, col_here * per_block, per_block, 1) - col_here * local_tiles
    )
    place = jnp.stack([row_here, col_here]).astype(jnp.int32)
    block, turned = assemble_call(place, row_tiles, col_tiles, block, landed)
    order = block.shape[0]
    diag = broadcast(block, ("row", "col"), 0)
    left = block.reshape(col_count, order // col_count, order)
    left = lax.all_to_all(left, "col", split_axis=0, concat_axis=0, tiled=True)
    top = turned.reshape(row_count, order // row_count, order)
    top = lax.all_to_all(top, "row", split_axis=0, concat_axis=0, tiled=True)
    corner, hi, lo, inv_hi, inv_lo = corner_call(diag)
    part = solve_call(left[0], top[0], hi, lo, inv_hi, inv_lo)
    across, down = gather_call(part, order, row_count, col_count)
    result = finish_call(place, block, across, down, corner)
    return (factor[None], result[None])


def solution(mesh):
    in_specs = (
        P(("front", "row", "col"), None, None),
        P("front", "row", "col"),
        P(("front", "row", "col"), None),
        P(("front", "row", "col")),
    )
    out_specs = (P(("front", "row", "col"), None, None), P("front", "row", "col"))
    return jax.shard_map(local, mesh=mesh, in_specs=in_specs, out_specs=out_specs, check_vma=False)
```

```python
import functools

import jax
import jax.numpy as jnp
from jax import lax
from jax.experimental import pallas as pl
from jax.experimental.pallas import tpu as pltpu
from jax.sharding import PartitionSpec as P

TILE = 128
NB = 16
F32 = jnp.float32
BF16 = jnp.bfloat16
NT = (((1,), (1,)), ((), ()))
TN = (((0,), (0,)), ((), ()))
PARAMS = pltpu.CompilerParams(vmem_limit_bytes=56 * 1024 * 1024)
VMEM = pl.BlockSpec(memory_space=pltpu.VMEM)
SMEM = pl.BlockSpec(memory_space=pltpu.SMEM)


def split(x):
    hi = x.astype(BF16)
    return hi, (x - hi.astype(F32)).astype(BF16)


def mxu(a, b, dims):
    return lax.dot_general(a, b, dims, preferred_element_type=F32)


def weights(hi, lo):
    top = jnp.concatenate([hi, hi], 1)
    return jnp.concatenate([top, jnp.concatenate([lo, jnp.zeros_like(lo)], 1)], 0)


def product(hi, lo, weight):
    both = mxu(jnp.concatenate([hi, lo], 1), weight, NT)
    return both[:, :TILE] + both[:, TILE:]


def product3(ah, al, bh, bl):
    return mxu(ah, bh, NT) + mxu(ah, bl, NT) + mxu(al, bh, NT)


def chol_inverse(work):
    rows = lax.broadcasted_iota(jnp.int32, (NB, TILE), 0)
    for start in range(0, TILE, NB):
        left = work[start : start + NB, :TILE]
        right = work[start : start + NB, TILE:]
        cols = [
            jnp.broadcast_to(left[:, start + b : start + b + 1], (NB, TILE)) for b in range(NB)
        ]
        for a in range(NB):
            scale = lax.rsqrt(cols[a][a : a + 1, :])
            factor = jnp.where(rows > a, cols[a] * scale, 0.0)
            pivot_left = left[a : a + 1, :] * scale
            pivot_right = right[a : a + 1, :] * scale
            left = jnp.where(rows == a, pivot_left, left - factor * pivot_left)
            right = jnp.where(rows == a, pivot_right, right - factor * pivot_right)
            for b in range(a + 1, NB):
                cols[b] = cols[b] - factor * (cols[b][a : a + 1, :] * scale)
        work[start : start + NB, :TILE] = left
        work[start : start + NB, TILE:] = right
        if start + NB < TILE:
            hi, lo = split(jnp.concatenate([left, right], 1))
            mine = jnp.concatenate([hi[:, :TILE], hi[:, :TILE], lo[:, :TILE]], 0)
            change = mxu(mine, jnp.concatenate([hi, lo, hi], 0), TN)
            work[start + NB :, :] = work[start + NB :, :] - change[start + NB :, :]


def factor_loop(src, out, hi, lo, inv_hi, inv_lo, work, col, blocks, chunk):
    total = src.shape[0]
    row_id = lax.broadcasted_iota(jnp.int32, (TILE, TILE), 0)
    col_id = lax.broadcasted_iota(jnp.int32, (TILE, TILE), 1)

    def step(k, carry):
        here = pl.ds(pl.multiple_of(k * TILE, TILE), TILE)
        col[...] = src[:, here]

        def earlier(m, carry):
            there = pl.ds(pl.multiple_of(m * TILE, TILE), TILE)
            weight = weights(hi[here, there], lo[here, there])
            for first in range(0, total, chunk):
                part = pl.ds(first, chunk)
                col[part, :] = col[part, :] - product(hi[part, there], lo[part, there], weight)
            return carry

        lax.fori_loop(0, k, earlier, 0)
        work[:, :TILE] = col[here, :]
        work[:, TILE:] = jnp.where(row_id == col_id, 1.0, 0.0).astype(F32)
        chol_inverse(work)
        inverse_hi, inverse_lo = split(work[:, TILE:])
        if inv_hi is not None:
            inv_hi[k] = inverse_hi
            inv_lo[k] = inverse_lo
        weight = weights(inverse_hi, inverse_lo)
        for first in range(0, total, chunk):
            part = pl.ds(first, chunk)
            a_hi, a_lo = split(col[part, :])
            panel = product(a_hi, a_lo, weight)
            ids = lax.broadcasted_iota(jnp.int32, (chunk, TILE), 0) + first
            panel = jnp.where(ids >= k * TILE, panel, 0.0)
            out[part, here] = panel
            p_hi, p_lo = split(panel)
            hi[part, here] = p_hi
            lo[part, here] = p_lo
        lower = jnp.where(row_id >= col_id, work[:, :TILE].T, 0.0)
        out[here, here] = lower
        d_hi, d_lo = split(lower)
        hi[here, here] = d_hi
        lo[here, here] = d_lo
        return carry

    lax.fori_loop(0, blocks, step, 0)


def child_kernel(row_count, col_count, front, factor, pieces, hi, lo, work, col):
    pivots = factor.shape[1]
    factor_loop(front, factor, hi, lo, None, None, work, col, pivots // TILE, 512)
    size = pieces.shape[1]

    def piece(index, carry):
        i = index // col_count
        j = index % col_count
        a = pl.ds(pl.multiple_of(pivots + i * size, TILE), size)
        b = pl.ds(pl.multiple_of(pivots + j * size, TILE), size)
        pieces[index] = front[a, b] - product3(hi[a, :], lo[a, :], hi[b, :], lo[b, :])
        return carry

    lax.fori_loop(0, row_count * col_count, piece, 0)


def child_call(front, border, row_count, col_count):
    order = front.shape[0]
    pivots = order - border
    size = border // row_count
    return pl.pallas_call(
        functools.partial(child_kernel, row_count, col_count),
        out_shape=(
            jax.ShapeDtypeStruct((order, pivots), F32),
            jax.ShapeDtypeStruct((row_count * col_count, size, size), F32),
        ),
        in_specs=[VMEM],
        out_specs=(VMEM, VMEM),
        scratch_shapes=[
            pltpu.VMEM((order, pivots), BF16),
            pltpu.VMEM((order, pivots), BF16),
            pltpu.VMEM((TILE, 2 * TILE), F32),
            pltpu.VMEM((order, TILE), F32),
        ],
        compiler_params=PARAMS,
        name="child",
    )(front)


def reorder_kernel(order, source, target):
    target[...] = source[...]


def reorder_call(order, pieces):
    shape = (1,) + pieces.shape[1:]
    return pl.pallas_call(
        reorder_kernel,
        out_shape=jax.ShapeDtypeStruct(pieces.shape, F32),
        grid_spec=pltpu.PrefetchScalarGridSpec(
            num_scalar_prefetch=1,
            grid=(pieces.shape[0],),
            in_specs=[pl.BlockSpec(shape, lambda i, order: (order[i], 0, 0))],
            out_specs=pl.BlockSpec(shape, lambda i, order: (i, 0, 0)),
        ),
        name="reorder",
    )(order, pieces)


def assemble_kernel(place, row_tiles, col_tiles, block, pieces, out, turned):
    out[...] = block[...]
    per_block = row_tiles.shape[1]

    def add(index, carry):
        for i in range(per_block):
            for j in range(per_block):
                r = pl.ds(pl.multiple_of(row_tiles[index, i] * TILE, TILE), TILE)
                c = pl.ds(pl.multiple_of(col_tiles[index, j] * TILE, TILE), TILE)
                tile = pieces[index, i * TILE : (i + 1) * TILE, j * TILE : (j + 1) * TILE]
                out[r, c] = out[r, c] + tile
        return carry

    lax.fori_loop(0, pieces.shape[0], add, 0)
    turned[...] = jnp.zeros_like(turned)

    @pl.when(place[0] == 0)
    def _():
        count = out.shape[0] // TILE

        def turn(k, carry):
            here = pl.ds(pl.multiple_of(k * TILE, TILE), TILE)
            for m in range(count):
                turned[m * TILE : (m + 1) * TILE, here] = out[here, m * TILE : (m + 1) * TILE].T
            return carry

        lax.fori_loop(0, count, turn, 0)


def assemble_call(place, row_tiles, col_tiles, block, pieces):
    return pl.pallas_call(
        assemble_kernel,
        out_shape=(jax.ShapeDtypeStruct(block.shape, F32),) * 2,
        in_specs=[SMEM, SMEM, SMEM, VMEM, VMEM],
        out_specs=(VMEM, VMEM),
        compiler_params=PARAMS,
        name="assemble",
    )(place, row_tiles, col_tiles, block, pieces)


def corner_kernel(src, out, hi, lo, inv_hi, inv_lo, work, col):
    factor_loop(
        src, out, hi, lo, inv_hi, inv_lo, work, col, src.shape[1] // TILE, src.shape[0] // 2
    )


def corner_call(src):
    order = src.shape[0]
    blocks = order // TILE
    return pl.pallas_call(
        corner_kernel,
        out_shape=(
            jax.ShapeDtypeStruct((order, order), F32),
            jax.ShapeDtypeStruct((order, order), BF16),
            jax.ShapeDtypeStruct((order, order), BF16),
            jax.ShapeDtypeStruct((blocks, TILE, TILE), BF16),
            jax.ShapeDtypeStruct((blocks, TILE, TILE), BF16),
        ),
        in_specs=[VMEM],
        out_specs=(VMEM,) * 5,
        scratch_shapes=[pltpu.VMEM((TILE, 2 * TILE), F32), pltpu.VMEM((order, TILE), F32)],
        compiler_params=PARAMS,
        name="corner",
    )(src)


def solve_kernel(left, top, hi, lo, inv_hi, inv_lo, panel, p_hi, p_lo):
    count = hi.shape[0] // TILE
    share = left.shape[0]
    panel[:share, :] = left[...]
    panel[share:, :] = top[...]

    def step(k, carry):
        here = pl.ds(pl.multiple_of(k * TILE, TILE), TILE)

        def earlier(m, carry):
            there = pl.ds(pl.multiple_of(m * TILE, TILE), TILE)
            weight = weights(hi[here, there], lo[here, there])
            panel[:, here] = panel[:, here] - product(p_hi[:, there], p_lo[:, there], weight)
            return carry

        lax.fori_loop(0, k, earlier, 0)
        a_hi, a_lo = split(panel[:, here])
        solved = product(a_hi, a_lo, weights(inv_hi[k], inv_lo[k]))
        panel[:, here] = solved
        s_hi, s_lo = split(solved)
        p_hi[:, here] = s_hi
        p_lo[:, here] = s_lo
        return carry

    lax.fori_loop(0, count, step, 0)


def solve_call(left, top, hi, lo, inv_hi, inv_lo):
    shape = (left.shape[0] + top.shape[0], left.shape[1])
    return pl.pallas_call(
        solve_kernel,
        out_shape=jax.ShapeDtypeStruct(shape, F32),
        in_specs=[VMEM] * 6,
        out_specs=VMEM,
        scratch_shapes=[pltpu.VMEM(shape, BF16), pltpu.VMEM(shape, BF16)],
        compiler_params=PARAMS,
        name="solve",
    )(left, top, hi, lo, inv_hi, inv_lo)


def gather_kernel(rows, cols, part, row_out, col_out, own, send_row, get_row, send_col, get_col):
    row = lax.axis_index("row")
    column = lax.axis_index("col")
    share = part.shape[0] - row_out.shape[0] // cols
    first = part.shape[0] - share
    barrier = pltpu.get_barrier_semaphore()
    for step in range(1, cols):
        peer = {"col": lax.rem(column + step, cols)}
        pl.semaphore_signal(barrier, inc=1, device_id=peer, device_id_type=pl.DeviceIdType.MESH)
    for step in range(1, rows):
        peer = {"row": lax.rem(row + step, rows)}
        pl.semaphore_signal(barrier, inc=1, device_id=peer, device_id_type=pl.DeviceIdType.MESH)
    pl.semaphore_wait(barrier, cols + rows - 2)
    copies = []
    for step in range(1, cols):
        copies.append(
            pltpu.make_async_remote_copy(
                src_ref=part.at[pl.ds(0, first)],
                dst_ref=row_out.at[pl.ds(pl.multiple_of(column * first, first), first)],
                send_sem=send_row.at[step - 1],
                recv_sem=get_row.at[step - 1],
                device_id={"col": lax.rem(column + step, cols)},
                device_id_type=pl.DeviceIdType.MESH,
            )
        )
    for step in range(1, rows):
        copies.append(
            pltpu.make_async_remote_copy(
                src_ref=part.at[pl.ds(first, share)],
                dst_ref=col_out.at[pl.ds(pl.multiple_of(row * share, share), share)],
                send_sem=send_col.at[step - 1],
                recv_sem=get_col.at[step - 1],
                device_id={"row": lax.rem(row + step, rows)},
                device_id_type=pl.DeviceIdType.MESH,
            )
        )
    for copy in copies:
        copy.start()
    mine = (
        pltpu.make_async_copy(
            part.at[pl.ds(0, first)],
            row_out.at[pl.ds(pl.multiple_of(column * first, first), first)],
            own.at[0],
        ),
        pltpu.make_async_copy(
            part.at[pl.ds(first, share)],
            col_out.at[pl.ds(pl.multiple_of(row * share, share), share)],
            own.at[1],
        ),
    )
    for copy in mine:
        copy.start()
    for copy in mine:
        copy.wait()
    for copy in copies:
        copy.wait()


def gather_call(part, order, rows, cols):
    anywhere = pl.BlockSpec(memory_space=pl.ANY)
    return pl.pallas_call(
        functools.partial(gather_kernel, rows, cols),
        out_shape=(jax.ShapeDtypeStruct((order, order), F32),) * 2,
        in_specs=[anywhere],
        out_specs=(anywhere, anywhere),
        scratch_shapes=[
            pltpu.SemaphoreType.DMA((2,)),
            pltpu.SemaphoreType.DMA((cols - 1,)),
            pltpu.SemaphoreType.DMA((cols - 1,)),
            pltpu.SemaphoreType.DMA((rows - 1,)),
            pltpu.SemaphoreType.DMA((rows - 1,)),
        ],
        compiler_params=pltpu.CompilerParams(
            collective_id=1, has_side_effects=True, vmem_limit_bytes=32 * 1024 * 1024
        ),
        name="gather",
    )(part)


def finish_kernel(place, block, across, down, corner, out):
    order = block.shape[0]
    count = order // TILE
    row = place[0]
    column = place[1]

    @pl.when((row == 0) & (column == 0))
    def _():
        out[...] = corner[...]

    @pl.when((row > 0) & (column == 0))
    def _():
        out[...] = across[...]

    @pl.when((row == 0) & (column > 0))
    def _():
        def back(k, carry):
            here = pl.ds(pl.multiple_of(k * TILE, TILE), TILE)
            for m in range(count):
                out[here, m * TILE : (m + 1) * TILE] = down[m * TILE : (m + 1) * TILE, here].T
            return carry

        lax.fori_loop(0, count, back, 0)

    @pl.when((row > 0) & (column > 0))
    def _():
        size = 2 * TILE
        wide = order // size

        def trail(index, carry):
            a = pl.ds(pl.multiple_of(index // wide * size, size), size)
            b = pl.ds(pl.multiple_of(index % wide * size, size), size)
            a_hi, a_lo = split(across[a, :])
            b_hi, b_lo = split(down[b, :])
            out[a, b] = block[a, b] - product3(a_hi, a_lo, b_hi, b_lo)
            return carry

        lax.fori_loop(0, wide * wide, trail, 0)


def finish_call(place, block, across, down, corner):
    return pl.pallas_call(
        finish_kernel,
        out_shape=jax.ShapeDtypeStruct(block.shape, F32),
        in_specs=[SMEM] + [VMEM] * 4,
        out_specs=VMEM,
        compiler_params=PARAMS,
        name="finish",
    )(place, block, across, down, corner)


def broadcast(array, axis, root):
    mine = lax.axis_index(axis) == root
    return lax.psum(jnp.where(mine, array, jnp.zeros_like(array)), axis)


def local(child_fronts, parent_entries, tile_map, parent_group):
    border_tiles = tile_map.shape[1]
    border = border_tiles * TILE
    row_count = lax.axis_size("row")
    col_count = lax.axis_size("col")
    front_count = lax.axis_size("front")
    row_here = lax.axis_index("row")
    col_here = lax.axis_index("col")
    front_here = lax.axis_index("front")
    group_size = row_count * col_count

    labels = jnp.concatenate([tile_map, parent_group[:, None]], 1)
    labels = lax.all_gather(labels, ("front", "row", "col"), axis=0, tiled=True)
    labels = labels.reshape(front_count, group_size, border_tiles + 1)
    groups = labels[:, :, border_tiles]
    number = jnp.arange(group_size, dtype=jnp.int32)
    ahead = (groups[:, None, :] < groups[:, :, None]) | (
        (groups[:, None, :] == groups[:, :, None]) & (number[None, None, :] < number[None, :, None])
    )
    rank = jnp.sum(ahead.astype(jnp.int32), 2)
    chosen = rank[:, None, :] == number[None, :, None]
    arrange = jnp.sum(jnp.where(chosen, number[None, None, :], 0), 2)
    per_parent = group_size // front_count
    ids = jnp.sum(
        jnp.where(chosen[:, :, :, None], labels[:, None, :, :border_tiles], 0), 2
    ).reshape(front_count, front_count, per_parent, border_tiles)
    ids = lax.dynamic_index_in_dim(ids, front_here, 1, False).reshape(-1, border_tiles)
    my_order = lax.dynamic_index_in_dim(arrange, front_here, 0, False)

    factor, pieces = child_call(child_fronts[0], border, row_count, col_count)
    size = border // row_count
    arrived = lax.all_to_all(pieces, ("row", "col"), split_axis=0, concat_axis=0, tiled=True)
    regrouped = reorder_call(my_order, arrived).reshape(front_count, per_parent, size, size)
    landed = lax.all_to_all(regrouped, "front", split_axis=0, concat_axis=0, tiled=True)
    landed = landed.reshape(-1, size, size)

    block = parent_entries[0]
    local_tiles = block.shape[0] // TILE
    per_block = border_tiles // row_count
    row_tiles = (
        lax.dynamic_slice_in_dim(ids, row_here * per_block, per_block, 1) - row_here * local_tiles
    )
    col_tiles = (
        lax.dynamic_slice_in_dim(ids, col_here * per_block, per_block, 1) - col_here * local_tiles
    )
    place = jnp.stack([row_here, col_here]).astype(jnp.int32)
    block, turned = assemble_call(place, row_tiles, col_tiles, block, landed)
    order = block.shape[0]
    diag = broadcast(block, ("row", "col"), 0)
    diag, block, turned = lax.optimization_barrier((diag, block, turned))
    left = block.reshape(col_count, order // col_count, order)
    left = lax.all_to_all(left, "col", split_axis=0, concat_axis=0, tiled=True)
    top = turned.reshape(row_count, order // row_count, order)
    top = lax.all_to_all(top, "row", split_axis=0, concat_axis=0, tiled=True)
    corner, hi, lo, inv_hi, inv_lo = corner_call(diag)
    part = solve_call(left[0], top[0], hi, lo, inv_hi, inv_lo)
    across, down = gather_call(part, order, row_count, col_count)
    result = finish_call(place, block, across, down, corner)
    return (factor[None], result[None])


def solution(mesh):
    in_specs = (
        P(("front", "row", "col"), None, None),
        P("front", "row", "col"),
        P(("front", "row", "col"), None),
        P(("front", "row", "col")),
    )
    out_specs = (P(("front", "row", "col"), None, None), P("front", "row", "col"))
    return jax.shard_map(local, mesh=mesh, in_specs=in_specs, out_specs=out_specs, check_vma=False)
```
